512 devices in a mesh: member: 16 (over y, core), grid: 32 (over x, z).
Axes of the slice: x: 4, y: 8, z: 8, core: 2. Of those that a mesh axis runs over, the one named last changes fastest.
Arguments:
- latents: bfloat16 [16, 1536, 1024], P('member', 'grid'), may hold values from -6 to 6
- dst_embed: bfloat16 [8192, 1024], P('grid'), may hold values from -6 to 6
- w_msg: bfloat16 [1024, 1024], replicated, may hold values from -0.1875 to 0.1875
- w_out: bfloat16 [1024, 128], replicated, may hold values from -0.1875 to 0.1875
- need_rows: int32 [96, 32], P('grid'), may hold values from 0 to 47, as said below
- edge_src: int32 [24576], P('grid'), may hold values from 0 to 95, as said below
- edge_dst: int32 [24576], P('grid'), may hold values from 0 to 255
- edge_count: int32 [32], P('grid'), may hold values from 96 to 768, as said below
- target: float32 [8192, 128], P('grid'), may hold values from -6 to 6
- point_weight: float32 [8192], P('grid')
- field_weight: float32 [128], replicated, may hold values from 0.3 to 3
Outputs:
- grad_latents: float32 [16, 1536, 1024], P('member', 'grid')
The draws below stay inside these ranges and needn't reach their ends.
Inputs may be any that keep to these rules, and one draw needn't show every extreme that they name: `need_rows`: row 3 g + r lists 32 distinct mesh nodes, as indices within shard (g + r - 1) mod 32, that grid shard g reads. `edge_src`: slot q of an edge reads request row q // 32 of its shard: 0 the shard before it, 1 its own, 2 the shard after it (cyclically). Grid shard g's first edge_count[g] edges are live and the rest are padding; some grid shard has all 768 live.
All inputs are finite; a program needn't handle non-finite values.
Results may differ from the reference program's by a relative error of at most 0.0095.
Values may be sent and summed in bfloat16 or wider, within the bound.
A program may use at most 64 MiB of HBM per device.

```python
import math
import jax
import jax.numpy as jnp
from jax import lax

D = 1024
F = 128
PTS_DEV = 256
NODE_DEV = 48
SLOTS = 32
EDGES_DEV = 768
MEMBERS = 16
NPTS = 8192
NODES = 1536
N_MEMBER = 16
N_GRID = 32


def draw_need_rows(key, part):
    key = jax.random.fold_in(key, 11)
    shards = NPTS // PTS_DEV
    offset = jax.random.randint(key, (shards * 3, 1), 0, NODE_DEV)
    return ((offset + jnp.arange(SLOTS, dtype=jnp.int32)[None, :]) % NODE_DEV).astype(jnp.int32)


def draw_edge_src(key, part):
    key = jax.random.fold_in(key, 14)
    shards = NPTS // PTS_DEV
    key_side, key_slot = jax.random.split(key)
    ticket = jax.random.randint(key_side, (shards * EDGES_DEV,), 0, 10)
    side = jnp.where(ticket < 2, 0, jnp.where(ticket >= 8, 2, 1))
    slot = jax.random.randint(key_slot, (shards * EDGES_DEV,), 0, SLOTS)
    return (side * SLOTS + slot).astype(jnp.int32)


def draw_edge_count(key, part):
    key = jax.random.fold_in(key, 12)
    shards = NPTS // PTS_DEV
    key_base, key_full = jax.random.split(key)
    base = EDGES_DEV // 8 + jax.random.randint(key_base, (shards,), 0, EDGES_DEV // 2 + 1)
    fullest = jax.random.randint(key_full, (), 0, shards)
    return jnp.where(jnp.arange(shards, dtype=jnp.int32) == fullest, EDGES_DEV, base).astype(jnp.int32)


def draw_point_weight(key, part):
    key = jax.random.fold_in(key, 13)
    shards = NPTS // PTS_DEV
    position = (jnp.arange(NPTS, dtype=jnp.int32) // PTS_DEV).astype(jnp.float32)
    rising = 1.0 + 2.0 * position / max(shards - 1, 1)
    rough = jnp.exp(jax.random.uniform(key, (NPTS,), jnp.float32, -0.6931, 0.6931))
    return (rising * rough).astype(jnp.float32)


def set_ends(drawn, stream_key, smallest, high):
    longest = drawn.shape.index(max(drawn.shape))
    spots = []
    for shift in (0, 1):
        where = [jax.random.randint(jax.random.fold_in(stream_key, axis), (), 0, length) for axis, length in enumerate(drawn.shape)]
        where[longest] = (where[longest] + shift) % drawn.shape[longest]
        spots.append(tuple(where))
    return drawn.at[spots[0]].set(smallest).at[spots[1]].set(high)


def steps_of(rng, shape, cuts, smallest, high):
    factor_of, own = 1.0, jax.random.fold_in(rng, 6)
    for axis_at, shards_of in cuts:
        heights = jnp.exp(jax.random.uniform(jax.random.fold_in(own, axis_at), (shards_of,), jnp.float32, smallest / len(cuts), high / len(cuts)))
        factor_of = factor_of * jnp.repeat(heights, shape[axis_at] // shards_of).reshape([-1 if axis == axis_at else 1 for axis in range(len(shape))])
    return factor_of


def normal_values(stream_key, shape, scale, bound, cuts=(), held_as=jnp.bfloat16):
    factor_of = steps_of(stream_key, shape, cuts, -0.22, 0.18) if cuts else 1.0
    values = jax.random.normal(stream_key, shape, jnp.float32) * scale * factor_of
    return jnp.minimum(jnp.maximum(values, -bound), bound).astype(held_as)


def setup_inputs(seed: int = 0) -> dict:
    keys = jax.random.split(jax.random.key(seed), 12)
    return {
        "latents": normal_values(keys[0], (MEMBERS, NODES, D), 1.0, 6.0, ((0, 16), (1, 32))),
        "dst_embed": normal_values(keys[1], (NPTS, D), 1.0, 6.0, ((0, 32),)),
        "w_msg": normal_values(keys[2], (D, D), D ** -0.5, 0.1875),
        "w_out": normal_values(keys[3], (D, F), D ** -0.5, 0.1875),
        "need_rows": draw_need_rows(jax.random.fold_in(keys[11], 71), 0),
        "edge_src": draw_edge_src(jax.random.fold_in(keys[11], 71), 0),
        "edge_dst": set_ends(jax.random.randint(keys[6], (N_GRID * EDGES_DEV,), 0, PTS_DEV), jax.random.fold_in(keys[6], 1), 0, PTS_DEV - 1).astype(jnp.int32),
        "edge_count": draw_edge_count(jax.random.fold_in(keys[11], 71), 0),
        "target": normal_values(keys[8], (NPTS, F), 1.0, 6.0, ((0, 32),), jnp.float32),
        "point_weight": draw_point_weight(jax.random.fold_in(keys[11], 71), 0),
        "field_weight": jnp.clip(jnp.exp(jax.random.uniform(keys[10], (F,), jnp.float32, math.log(0.3), math.log(3.0))), 0.3, 3.0),
    }


smooth_width = 0.1
norm_eps = 1e-06

def smooth_abs(gaps):
    return jnp.sqrt(gaps * gaps + smooth_width * smooth_width)

def smooth_slope(gaps):
    return gaps / smooth_abs(gaps)

def reference(latents, dst_embed, w_msg, w_out, need_rows, edge_src, edge_dst, edge_count, target, point_weight, field_weight):
    members = N_MEMBER
    edges_all = N_GRID * EDGES_DEV
    npoints = N_GRID * PTS_DEV
    order = jnp.arange(edges_all, dtype=jnp.int32)
    owner = order // EDGES_DEV
    live_col = (order % EDGES_DEV < edge_count[owner])[:, None]
    side = edge_src // SLOTS
    shard = (owner + side - 1 + N_GRID) % N_GRID
    source_node = shard * NODE_DEV + need_rows[owner * 3 + side, edge_src % SLOTS]
    dest_point = owner * PTS_DEV + edge_dst
    slot_seg = owner * (3 * SLOTS) + edge_src
    seg_all = jnp.arange(N_GRID * 3 * SLOTS, dtype=jnp.int32)
    seg_owner = seg_all // (3 * SLOTS)
    seg_side = seg_all // SLOTS % 3
    seg_node = (seg_owner + seg_side - 1 + N_GRID) % N_GRID * NODE_DEV + need_rows.reshape(-1)

    def forward(latent_rows):
        pre_act = latent_rows[source_node].astype(jnp.float32) + dst_embed[dest_point].astype(jnp.float32)
        hidden = jax.nn.silu(pre_act).astype(jnp.bfloat16)
        message = jnp.dot(hidden, w_msg, preferred_element_type=jnp.float32).astype(jnp.bfloat16)
        message = jnp.where(live_col, message, jnp.zeros((), jnp.bfloat16))
        summed = jax.ops.segment_sum(message.astype(jnp.float32), dest_point, num_segments=npoints)
        inv_rms = lax.rsqrt(lax.optimization_barrier(jnp.mean(summed * summed, axis=1, keepdims=True)) + norm_eps)
        unit_rows = summed * inv_rms
        normed = unit_rows.astype(jnp.bfloat16)
        fields = jnp.dot(normed, w_out, preferred_element_type=jnp.float32)
        return (pre_act, inv_rms, unit_rows, fields)
    fields_all = lax.map(lambda rows: forward(rows)[3], latents)

    def pairs(own):
        gaps = own[None] - fields_all
        return lax.optimization_barrier(jnp.sum(smooth_slope(gaps), axis=0))
    pair_slope = lax.map(pairs, fields_all)
    weights = point_weight[:, None] * field_weight[None, :]
    grads = weights[None] * (smooth_slope(fields_all - target[None]) - pair_slope / (members - 1))

    def backward(inputs):
        latent_rows, grad_fields = inputs
        pre_act, inv_rms, unit_rows, fields = forward(latent_rows)
        grad_cast = grad_fields.astype(jnp.bfloat16)
        grad_normed = lax.dot_general(grad_cast, w_out, (((1,), (1,)), ((), ())), preferred_element_type=jnp.float32)
        grad_summed = (inv_rms * (grad_normed - unit_rows * lax.optimization_barrier(jnp.mean(grad_normed * unit_rows, axis=1, keepdims=True)))).astype(jnp.bfloat16)
        grad_message = jnp.where(live_col, grad_summed[dest_point], jnp.zeros((), jnp.bfloat16))
        grad_hidden = lax.dot_general(grad_message, w_msg, (((1,), (1,)), ((), ())), preferred_element_type=jnp.float32)
        sigma = jax.nn.sigmoid(pre_act)
        grad_pre = (grad_hidden * sigma * (1.0 + pre_act * (1.0 - sigma))).astype(jnp.bfloat16)
        slot_grads = jax.ops.segment_sum(grad_pre.astype(jnp.float32), slot_seg, num_segments=N_GRID * 3 * SLOTS).astype(jnp.bfloat16)
        return jax.ops.segment_sum(slot_grads.astype(jnp.float32), seg_node, num_segments=N_GRID * NODE_DEV)
    grad_latents = lax.map(backward, (latents, grads))
    return grad_latents
```

```python
import functools

import jax
import jax.numpy as jnp
from jax import lax
from jax.experimental import pallas as pl
from jax.experimental.pallas import tpu as pltpu
from jax.sharding import PartitionSpec as P

smooth_width = 0.1
norm_eps = 1e-06

MESH = pl.DeviceIdType.MESH
NN = (((1,), (0,)), ((), ()))
NT = (((1,), (1,)), ((), ()))
F32 = jnp.float32
BF16 = jnp.bfloat16


def dot(a, b, dims=NN):
    return lax.dot_general(a, b, dims, preferred_element_type=F32)


def onehot(condition):
    return jnp.where(condition, 1.0, 0.0).astype(BF16)


def smooth_slope(gaps):
    return gaps * lax.rsqrt(gaps * gaps + smooth_width * smooth_width)


def sigmoid(v):
    return 0.5 * jnp.tanh(0.5 * v) + 0.5


def body(
    members,
    shards,
    lat_hbm,
    emb_hbm,
    wmsg_hbm,
    wout_hbm,
    need_hbm,
    src_hbm,
    dst_hbm,
    count_hbm,
    target_hbm,
    pw_hbm,
    fw_hbm,
    out_hbm,
    lat,
    emb,
    wmsg,
    wout,
    need,
    src,
    dst,
    count,
    truth,
    pw,
    fw,
    nbr,
    pre,
    od,
    odt,
    n_lr,
    nt,
    summed,
    normed,
    inv,
    fields,
    ens,
    gsend,
    gf,
    w2,
    u,
    rsend,
    own,
    back,
    out,
    pwcol,
    load_sem,
    lat_send,
    lat_recv,
    ens_send,
    ens_recv,
    gf_send,
    gf_recv,
    back_send,
    back_recv,
    out_sem,
):
    node_dev, width = lat.shape
    points = emb.shape[0]
    edges = src.shape[1]
    slots = need.shape[1]
    share = points // members
    chunk = 256
    chunks = width // chunk
    me = lax.axis_index("member")
    g = lax.axis_index("grid")
    left = lax.rem(g + shards - 1, shards)
    right = lax.rem(g + 1, shards)
    rows_me = pl.ds(pl.multiple_of(me * share, share), share)

    def cols(c):
        return pl.ds(c * chunk, chunk)

    loads = []
    for source, target in (
        (src_hbm, src),
        (dst_hbm, dst),
        (need_hbm, need),
        (count_hbm, count),
        (lat_hbm.at[0], lat),
        (emb_hbm, emb),
        (wmsg_hbm, wmsg),
        (wout_hbm, wout),
        (pw_hbm, pw),
        (fw_hbm, fw),
        (target_hbm.at[rows_me], truth),
    ):
        copy = pltpu.make_async_copy(source, target, load_sem.at[len(loads)])
        copy.start()
        loads.append(copy)

    barrier = pltpu.get_barrier_semaphore()
    for neighbour in (left, right):
        pl.semaphore_signal(barrier, inc=1, device_id={"grid": neighbour}, device_id_type=MESH)
    for d in range(1, members):
        pl.semaphore_signal(
            barrier, inc=1, device_id={"member": lax.rem(me + d, members)}, device_id_type=MESH
        )

    for copy in loads[:4]:
        copy.wait()
    lane = lax.broadcasted_iota(jnp.int32, (1, edges), 1)
    dest = jnp.where(lane < count[0], dst[...], -1)
    source = src[...]
    odt[...] = onehot(lax.broadcasted_iota(jnp.int32, (points, edges), 0) == dest)
    dest_col = jnp.transpose(jnp.broadcast_to(dest, (128, edges)))
    lanes = lax.broadcasted_iota(jnp.int32, (edges, 128), 1)
    for first in range(0, points, 128):
        od[:, first : first + 128] = onehot(dest_col == lanes + first)
    os_t = onehot(lax.broadcasted_iota(jnp.int32, (128, edges), 0) == source)
    os_n = onehot(jnp.transpose(jnp.broadcast_to(source, (128, edges))) == lanes)
    code = jnp.concatenate(
        [
            need[0:1, :],
            need[1:2, :] + 2 * node_dev,
            need[2:3, :] + node_dev,
            jnp.full((1, 128 - 3 * slots), -1, jnp.int32),
        ],
        axis=1,
    )
    place = onehot(lax.broadcasted_iota(jnp.int32, (3 * node_dev, 128), 0) == code)
    nt[...] = dot(place, os_t).astype(BF16)
    n_lr[...] = dot(os_n, place[: 2 * node_dev], NT).astype(BF16)
    n_own = dot(os_n, place[2 * node_dev :], NT).astype(BF16)

    loads[4].wait()
    pl.semaphore_wait(barrier, members + 1)
    lat_copies = []
    for c in range(chunks):
        for side, neighbour in ((1, left), (0, right)):
            copy = pltpu.make_async_remote_copy(
                src_ref=lat.at[:, cols(c)],
                dst_ref=nbr.at[pl.ds(side * node_dev, node_dev), cols(c)],
                send_sem=lat_send.at[side, c],
                recv_sem=lat_recv.at[side, c],
                device_id={"grid": neighbour},
                device_id_type=MESH,
            )
            copy.start()
            lat_copies.append(copy)

    loads[5].wait()
    for c in range(chunks):
        pre[:, cols(c)] = dot(od[...], emb[:, cols(c)]) + dot(n_own, lat[:, cols(c)])
    loads[6].wait()
    loads[7].wait()
    w2t = dot(wmsg[...], wout[...])
    high = w2t.astype(BF16)
    w2[:, :128] = high
    w2[:, 128:] = (w2t - high.astype(F32)).astype(BF16)
    for copy in loads[8:]:
        copy.wait()
    pwcol[...] = jnp.transpose(jnp.broadcast_to(pw[...], (128, points)))

    for c in range(chunks):
        for copy in lat_copies[2 * c : 2 * c + 2]:
            copy.wait_recv()
        v = pre[:, cols(c)] + dot(n_lr[...], nbr[:, cols(c)])
        pre[:, cols(c)] = v
        hidden = (v * sigmoid(v)).astype(BF16)
        gathered = dot(odt[...], hidden).astype(BF16)
        part = dot(gathered, wmsg[cols(c), :])
        if c == 0:
            summed[...] = part
        else:
            summed[...] += part
    total = summed[...]
    inv_rms = lax.rsqrt(jnp.mean(total * total, axis=1, keepdims=True) + norm_eps)
    inv[...] = inv_rms
    normed[...] = (total * inv_rms).astype(BF16)
    fields[...] = dot(normed[...], wout[...])

    ens_copies = []
    for d in range(1, members):
        other = lax.rem(me + d, members)
        copy = pltpu.make_async_remote_copy(
            src_ref=fields.at[pl.ds(pl.multiple_of(other * share, share), share)],
            dst_ref=ens.at[d - 1],
            send_sem=ens_send.at[d - 1],
            recv_sem=ens_recv.at[d - 1],
            device_id={"member": other},
            device_id_type=MESH,
        )
        copy.start()
        ens_copies.append(copy)

    for c in range(chunks):
        v = pre[:, cols(c)]
        s = sigmoid(v)
        pre[:, cols(c)] = s * (1.0 + v * (1.0 - s))
    u[...] = dot(normed[...], wmsg[...], NT)

    weights = pwcol[rows_me, :] * fw[...]
    for copy in ens_copies:
        copy.wait_recv()
    x = [fields[rows_me, :]] + [ens[d] for d in range(members - 1)]
    pair = [jnp.zeros_like(x[0]) for _ in x]
    for i in range(members):
        for j in range(i):
            slope = smooth_slope(x[i] - x[j])
            pair[i] = pair[i] + slope
            pair[j] = pair[j] - slope
    y = truth[...]
    grads = [
        (weights * (smooth_slope(x[i] - y) - pair[i] * (1.0 / (members - 1)))).astype(BF16)
        for i in range(members)
    ]
    gf_copies = []
    for d in range(1, members):
        gsend[d - 1] = grads[d]
        copy = pltpu.make_async_remote_copy(
            src_ref=gsend.at[d - 1],
            dst_ref=gf.at[rows_me],
            send_sem=gf_send.at[d - 1],
            recv_sem=gf_recv.at[d - 1],
            device_id={"member": lax.rem(me + members - d, members)},
            device_id_type=MESH,
        )
        copy.start()
        gf_copies.append(copy)
    gf[rows_me, :] = grads[0]
    for copy in gf_copies:
        copy.wait_recv()

    got = gf[...]
    along = jnp.sum(got.astype(F32) * fields[...], axis=1, keepdims=True) * (1.0 / width)
    twice = jnp.concatenate([got, got], axis=1)
    inv_rms = inv[...]
    back_copies = []
    for c in range(chunks):
        grad = inv_rms * (dot(twice, w2[cols(c), :], NT) - along * u[:, cols(c)])
        grad_pre = (dot(od[...], grad.astype(BF16)) * pre[:, cols(c)]).astype(BF16)
        rows = dot(nt[...], grad_pre)
        rsend[:, cols(c)] = rows[: 2 * node_dev].astype(BF16)
        own[:, cols(c)] = rows[2 * node_dev :]
        for side, neighbour in ((0, left), (1, right)):
            copy = pltpu.make_async_remote_copy(
                src_ref=rsend.at[pl.ds(side * node_dev, node_dev), cols(c)],
                dst_ref=back.at[side, :, cols(c)],
                send_sem=back_send.at[side, c],
                recv_sem=back_recv.at[side, c],
                device_id={"grid": neighbour},
                device_id_type=MESH,
            )
            copy.start()
            back_copies.append(copy)
    stores = []
    for c in range(chunks):
        for copy in back_copies[2 * c : 2 * c + 2]:
            copy.wait_recv()
        out[:, cols(c)] = (
            own[:, cols(c)] + back[0, :, cols(c)].astype(F32) + back[1, :, cols(c)].astype(F32)
        )
        copy = pltpu.make_async_copy(out.at[:, cols(c)], out_hbm.at[0, :, cols(c)], out_sem.at[c])
        copy.start()
        stores.append(copy)
    for copy in lat_copies + ens_copies + gf_copies + back_copies:
        copy.wait_send()
    for copy in stores:
        copy.wait()


def local(
    latents,
    dst_embed,
    w_msg,
    w_out,
    need_rows,
    edge_src,
    edge_dst,
    edge_count,
    target,
    point_weight,
    field_weight,
):
    members = lax.axis_size("member")
    shards = lax.axis_size("grid")
    node_dev, width = latents.shape[1:]
    points = dst_embed.shape[0]
    edges = edge_src.shape[0]
    fields = w_out.shape[1]
    share = points // members
    chunks = width // 256
    dma = pltpu.SemaphoreType.DMA
    return pl.pallas_call(
        functools.partial(body, members, shards),
        out_shape=jax.ShapeDtypeStruct((1, node_dev, width), F32),
        in_specs=[pl.BlockSpec(memory_space=pl.ANY)] * 11,
        out_specs=pl.BlockSpec(memory_space=pl.ANY),
        scratch_shapes=[
            pltpu.VMEM((node_dev, width), BF16),
            pltpu.VMEM((points, width), BF16),
            pltpu.VMEM((width, width), BF16),
            pltpu.VMEM((width, fields), BF16),
            pltpu.VMEM(need_rows.shape, jnp.int32),
            pltpu.VMEM((1, edges), jnp.int32),
            pltpu.VMEM((1, edges), jnp.int32),
            pltpu.SMEM((1,), jnp.int32),
            pltpu.VMEM((share, fields), F32),
            pltpu.VMEM((1, points), F32),
            pltpu.VMEM((1, fields), F32),
            pltpu.VMEM((2 * node_dev, width), BF16),
            pltpu.VMEM((edges, width), F32),
            pltpu.VMEM((edges, points), BF16),
            pltpu.VMEM((points, edges), BF16),
            pltpu.VMEM((edges, 2 * node_dev), BF16),
            pltpu.VMEM((3 * node_dev, edges), BF16),
            pltpu.VMEM((points, width), F32),
            pltpu.VMEM((points, width), BF16),
            pltpu.VMEM((points, 1), F32),
            pltpu.VMEM((points, fields), F32),
            pltpu.VMEM((members - 1, share, fields), F32),
            pltpu.VMEM((members - 1, share, fields), BF16),
            pltpu.VMEM((points, fields), BF16),
            pltpu.VMEM((width, 2 * fields), BF16),
            pltpu.VMEM((points, width), F32),
            pltpu.VMEM((2 * node_dev, width), BF16),
            pltpu.VMEM((node_dev, width), F32),
            pltpu.VMEM((2, node_dev, width), BF16),
            pltpu.VMEM((node_dev, width), F32),
            pltpu.VMEM((points, 128), F32),
            dma((11,)),
            dma((2, chunks)),
            dma((2, chunks)),
            dma((members - 1,)),
            dma((members - 1,)),
            dma((members - 1,)),
            dma((members - 1,)),
            dma((2, chunks)),
            dma((2, chunks)),
            dma((chunks,)),
        ],
        compiler_params=pltpu.CompilerParams(
            collective_id=0, has_side_effects=True, vmem_limit_bytes=48 * 1024 * 1024
        ),
        cost_estimate=pl.CostEstimate(
            flops=6_000_000_000, bytes_accessed=4_000_000, transcendentals=1_600_000
        ),
    )(
        latents,
        dst_embed,
        w_msg,
        w_out,
        need_rows,
        edge_src[None],
        edge_dst[None],
        edge_count,
        target,
        point_weight[None],
        field_weight[None],
    )


def solution(mesh):
    placed = (
        P("member", "grid", None),
        P("grid", None),
        P(),
        P(),
        P("grid", None),
        P("grid"),
        P("grid"),
        P("grid"),
        P("grid", None),
        P("grid"),
        P(),
    )
    return jax.shard_map(
        local, mesh=mesh, in_specs=placed, out_specs=P("member", "grid", None), check_vma=False
    )
```

```python
import functools

import jax
import jax.numpy as jnp
from jax import lax
from jax.experimental import pallas as pl
from jax.experimental.pallas import tpu as pltpu
from jax.sharding import PartitionSpec as P

smooth_width = 0.1
norm_eps = 1e-06

MESH = pl.DeviceIdType.MESH
NN = (((1,), (0,)), ((), ()))
NT = (((1,), (1,)), ((), ()))
F32 = jnp.float32
BF16 = jnp.bfloat16


def dot(a, b, dims=NN):
    return lax.dot_general(a, b, dims, preferred_element_type=F32)


def onehot(condition):
    return jnp.where(condition, 1.0, 0.0).astype(BF16)


def smooth_slope(gaps):
    return gaps * lax.rsqrt(gaps * gaps + smooth_width * smooth_width)


def sigmoid(v):
    return 0.5 * jnp.tanh(0.5 * v) + 0.5


def body(
    members,
    shards,
    lat_hbm,
    emb_hbm,
    wmsg_hbm,
    wout_hbm,
    need_hbm,
    src_hbm,
    dst_hbm,
    count_hbm,
    target_hbm,
    pw_hbm,
    fw_hbm,
    out,
    lat,
    emb,
    wmsg,
    wout,
    need,
    src,
    dst,
    count,
    truth,
    pw,
    fw,
    nbr,
    pre,
    od,
    odt,
    n_lr,
    nt,
    summed,
    normed,
    inv,
    fields,
    ens,
    gsend,
    gf,
    w2,
    u,
    rsend,
    own,
    back,
    pwcol,
    load_sem,
    lat_send,
    lat_recv,
    ens_send,
    ens_recv,
    gf_send,
    gf_recv,
    back_send,
    back_recv,
):
    node_dev, width = lat.shape
    points = emb.shape[0]
    edges = src.shape[0]
    slots = need.shape[1]
    share = points // members
    chunk = 256
    chunks = width // chunk
    me = lax.axis_index("member")
    g = lax.axis_index("grid")
    left = lax.rem(g + shards - 1, shards)
    right = lax.rem(g + 1, shards)
    rows_me = pl.ds(pl.multiple_of(me * share, share), share)

    order = sorted(range(1, members), key=lambda d: -min(d, members - d))

    def cols(c):
        return pl.ds(c * chunk, chunk)

    barrier = pltpu.get_barrier_semaphore()
    for neighbour in (left, right):
        pl.semaphore_signal(barrier, inc=1, device_id={"grid": neighbour}, device_id_type=MESH)
    for d in order:
        pl.semaphore_signal(
            barrier, inc=1, device_id={"member": lax.rem(me + d, members)}, device_id_type=MESH
        )

    loads = []
    for source, target in (
        (src_hbm, src),
        (dst_hbm, dst),
        (need_hbm, need),
        (count_hbm, count),
        (lat_hbm.at[0], lat),
        (emb_hbm, emb),
        (wmsg_hbm, wmsg),
        (wout_hbm, wout),
        (pw_hbm, pw),
        (fw_hbm, fw),
        (target_hbm.at[rows_me], truth),
    ):
        copy = pltpu.make_async_copy(source, target, load_sem.at[len(loads)])
        copy.start()
        loads.append(copy)

    for copy in loads[:4]:
        copy.wait()
    lane = lax.broadcasted_iota(jnp.int32, (1, edges), 1)
    dest = jnp.where(lane < count[0], dst[...].reshape(1, edges), -1)
    source = src[...].reshape(1, edges)
    odt[...] = onehot(lax.broadcasted_iota(jnp.int32, (points, edges), 0) == dest)
    dest_col = jnp.transpose(jnp.broadcast_to(dest, (128, edges)))
    lanes = lax.broadcasted_iota(jnp.int32, (edges, 128), 1)
    for first in range(0, points, 128):
        od[:, first : first + 128] = onehot(dest_col == lanes + first)
    os_t = onehot(lax.broadcasted_iota(jnp.int32, (128, edges), 0) == source)
    os_n = onehot(jnp.transpose(jnp.broadcast_to(source, (128, edges))) == lanes)
    code = jnp.concatenate(
        [
            need[0:1, :],
            need[1:2, :] + 2 * node_dev,
            need[2:3, :] + node_dev,
            jnp.full((1, 128 - 3 * slots), -1, jnp.int32),
        ],
        axis=1,
    )
    place = onehot(lax.broadcasted_iota(jnp.int32, (3 * node_dev, 128), 0) == code)
    nt[...] = dot(place, os_t).astype(BF16)
    n_lr[...] = dot(os_n, place[: 2 * node_dev], NT).astype(BF16)
    n_own = dot(os_n, place[2 * node_dev :], NT).astype(BF16)

    loads[4].wait()
    pl.semaphore_wait(barrier, members + 1)
    lat_copies = []
    for c in range(chunks):
        for side, neighbour in ((1, left), (0, right)):
            copy = pltpu.make_async_remote_copy(
                src_ref=lat.at[:, cols(c)],
                dst_ref=nbr.at[pl.ds(side * node_dev, node_dev), cols(c)],
                send_sem=lat_send.at[side, c],
                recv_sem=lat_recv.at[side, c],
                device_id={"grid": neighbour},
                device_id_type=MESH,
            )
            copy.start()
            lat_copies.append(copy)

    loads[5].wait()
    for c in range(chunks):
        pre[:, cols(c)] = dot(od[...], emb[:, cols(c)]) + dot(n_own, lat[:, cols(c)])
    loads[6].wait()
    loads[7].wait()
    w2t = dot(wmsg[...], wout[...])
    high = w2t.astype(BF16)
    w2[:, :128] = high
    w2[:, 128:] = (w2t - high.astype(F32)).astype(BF16)
    for copy in loads[8:]:
        copy.wait()
    pwcol[...] = jnp.transpose(jnp.broadcast_to(pw[...].reshape(1, points), (128, points)))

    for c in range(chunks):
        for copy in lat_copies[2 * c : 2 * c + 2]:
            copy.wait_recv()
        v = pre[:, cols(c)] + dot(n_lr[...], nbr[:, cols(c)])
        pre[:, cols(c)] = v
        hidden = (v * sigmoid(v)).astype(BF16)
        gathered = dot(odt[...], hidden).astype(BF16)
        part = dot(gathered, wmsg[cols(c), :])
        if c == 0:
            summed[...] = part
        else:
            summed[...] += part
    total = summed[...]
    inv_rms = lax.rsqrt(jnp.mean(total * total, axis=1, keepdims=True) + norm_eps)
    inv[...] = inv_rms
    normed[...] = (total * inv_rms).astype(BF16)
    fields[...] = dot(normed[...], wout[...])

    ens_copies = []
    for d in order:
        other = lax.rem(me + d, members)
        copy = pltpu.make_async_remote_copy(
            src_ref=fields.at[pl.ds(pl.multiple_of(other * share, share), share)],
            dst_ref=ens.at[d - 1],
            send_sem=ens_send.at[d - 1],
            recv_sem=ens_recv.at[d - 1],
            device_id={"member": other},
            device_id_type=MESH,
        )
        copy.start()
        ens_copies.append(copy)

    for c in range(chunks):
        v = pre[:, cols(c)]
        s = sigmoid(v)
        pre[:, cols(c)] = s * (1.0 + v * (1.0 - s))
    u[...] = dot(normed[...], wmsg[...], NT)

    weights = pwcol[rows_me, :] * fw[...].reshape(1, fw.shape[0])
    for copy in ens_copies:
        copy.wait_recv()
    x = [fields[rows_me, :]] + [ens[d] for d in range(members - 1)]
    pair = [jnp.zeros_like(x[0]) for _ in x]
    for i in range(members):
        for j in range(i):
            slope = smooth_slope(x[i] - x[j])
            pair[i] = pair[i] + slope
            pair[j] = pair[j] - slope
    y = truth[...]
    grads = [
        (weights * (smooth_slope(x[i] - y) - pair[i] * (1.0 / (members - 1)))).astype(BF16)
        for i in range(members)
    ]
    gf_copies = []
    for d in order:
        gsend[d - 1] = grads[d]
        copy = pltpu.make_async_remote_copy(
            src_ref=gsend.at[d - 1],
            dst_ref=gf.at[rows_me],
            send_sem=gf_send.at[d - 1],
            recv_sem=gf_recv.at[d - 1],
            device_id={"member": lax.rem(me + members - d, members)},
            device_id_type=MESH,
        )
        copy.start()
        gf_copies.append(copy)
    gf[rows_me, :] = grads[0]
    for copy in gf_copies:
        copy.wait_recv()

    got = gf[...]
    along = jnp.sum(got.astype(F32) * fields[...], axis=1, keepdims=True) * (1.0 / width)
    twice = jnp.concatenate([got, got], axis=1)
    inv_rms = inv[...]
    back_copies = []
    for c in range(chunks):
        grad = inv_rms * (dot(twice, w2[cols(c), :], NT) - along * u[:, cols(c)])
        grad_pre = (dot(od[...], grad.astype(BF16)) * pre[:, cols(c)]).astype(BF16)
        rows = dot(nt[...], grad_pre)
        rsend[:, cols(c)] = rows[: 2 * node_dev].astype(BF16)
        own[:, cols(c)] = rows[2 * node_dev :]
        for side, neighbour in ((0, left), (1, right)):
            copy = pltpu.make_async_remote_copy(
                src_ref=rsend.at[pl.ds(side * node_dev, node_dev), cols(c)],
                dst_ref=back.at[side, :, cols(c)],
                send_sem=back_send.at[side, c],
                recv_sem=back_recv.at[side, c],
                device_id={"grid": neighbour},
                device_id_type=MESH,
            )
            copy.start()
            back_copies.append(copy)
    for c in range(chunks):
        for copy in back_copies[2 * c : 2 * c + 2]:
            copy.wait_recv()
        out[0, :, cols(c)] = (
            own[:, cols(c)] + back[0, :, cols(c)].astype(F32) + back[1, :, cols(c)].astype(F32)
        )
    for copy in lat_copies + ens_copies + gf_copies + back_copies:
        copy.wait_send()


def local(
    latents,
    dst_embed,
    w_msg,
    w_out,
    need_rows,
    edge_src,
    edge_dst,
    edge_count,
    target,
    point_weight,
    field_weight,
):
    members = lax.axis_size("member")
    shards = lax.axis_size("grid")
    node_dev, width = latents.shape[1:]
    points = dst_embed.shape[0]
    edges = edge_src.shape[0]
    fields = w_out.shape[1]
    share = points // members
    chunks = width // 256
    dma = pltpu.SemaphoreType.DMA
    return pl.pallas_call(
        functools.partial(body, members, shards),
        out_shape=pltpu.VMEM((1, node_dev, width), F32),
        in_specs=[pl.BlockSpec(memory_space=pl.ANY)] * 11,
        out_specs=pl.BlockSpec(memory_space=pltpu.VMEM),
        scratch_shapes=[
            pltpu.VMEM((node_dev, width), BF16),
            pltpu.VMEM((points, width), BF16),
            pltpu.VMEM((width, width), BF16),
            pltpu.VMEM((width, fields), BF16),
            pltpu.VMEM(need_rows.shape, jnp.int32),
            pltpu.VMEM((edges,), jnp.int32),
            pltpu.VMEM((edges,), jnp.int32),
            pltpu.SMEM((1,), jnp.int32),
            pltpu.VMEM((share, fields), F32),
            pltpu.VMEM((points,), F32),
            pltpu.VMEM((fields,), F32),
            pltpu.VMEM((2 * node_dev, width), BF16),
            pltpu.VMEM((edges, width), F32),
            pltpu.VMEM((edges, points), BF16),
            pltpu.VMEM((points, edges), BF16),
            pltpu.VMEM((edges, 2 * node_dev), BF16),
            pltpu.VMEM((3 * node_dev, edges), BF16),
            pltpu.VMEM((points, width), F32),
            pltpu.VMEM((points, width), BF16),
            pltpu.VMEM((points, 1), F32),
            pltpu.VMEM((points, fields), F32),
            pltpu.VMEM((members - 1, share, fields), F32),
            pltpu.VMEM((members - 1, share, fields), BF16),
            pltpu.VMEM((points, fields), BF16),
            pltpu.VMEM((width, 2 * fields), BF16),
            pltpu.VMEM((points, width), F32),
            pltpu.VMEM((2 * node_dev, width), BF16),
            pltpu.VMEM((node_dev, width), F32),
            pltpu.VMEM((2, node_dev, width), BF16),
            pltpu.VMEM((points, 128), F32),
            dma((11,)),
            dma((2, chunks)),
            dma((2, chunks)),
            dma((members - 1,)),
            dma((members - 1,)),
            dma((members - 1,)),
            dma((members - 1,)),
            dma((2, chunks)),
            dma((2, chunks)),
        ],
        compiler_params=pltpu.CompilerParams(
            collective_id=0, has_side_effects=True, vmem_limit_bytes=32 * 1024 * 1024
        ),
        cost_estimate=pl.CostEstimate(
            flops=6_000_000_000, bytes_accessed=4_000_000, transcendentals=1_600_000
        ),
    )(
        pltpu.with_memory_space_constraint(latents, pltpu.HBM),
        pltpu.with_memory_space_constraint(dst_embed, pltpu.HBM),
        pltpu.with_memory_space_constraint(w_msg, pltpu.HBM),
        pltpu.with_memory_space_constraint(w_out, pltpu.HBM),
        pltpu.with_memory_space_constraint(need_rows, pltpu.HBM),
        pltpu.with_memory_space_constraint(edge_src, pltpu.HBM),
        pltpu.with_memory_space_constraint(edge_dst, pltpu.HBM),
        edge_count,
        pltpu.with_memory_space_constraint(target, pltpu.HBM),
        pltpu.with_memory_space_constraint(point_weight, pltpu.HBM),
        pltpu.with_memory_space_constraint(field_weight, pltpu.HBM),
    )


def solution(mesh):
    placed = (
        P("member", "grid", None),
        P("grid", None),
        P(),
        P(),
        P("grid", None),
        P("grid"),
        P("grid"),
        P("grid"),
        P("grid", None),
        P("grid"),
        P(),
    )
    return jax.shard_map(
        local, mesh=mesh, in_specs=placed, out_specs=P("member", "grid", None), check_vma=False
    )
```

```python
import functools

import jax
import jax.numpy as jnp
from jax import lax
from jax.experimental import pallas as pl
from jax.experimental.pallas import tpu as pltpu
from jax.sharding import PartitionSpec as P

smooth_width = 0.1
norm_eps = 1e-06

MESH = pl.DeviceIdType.MESH
NN = (((1,), (0,)), ((), ()))
NT = (((1,), (1,)), ((), ()))
F32 = jnp.float32
BF16 = jnp.bfloat16


def dot(a, b, dims=NN):
    return lax.dot_general(a, b, dims, preferred_element_type=F32)


def onehot(condition):
    return jnp.where(condition, 1.0, 0.0).astype(BF16)


def smooth_slope(gaps):
    return gaps * lax.rsqrt(gaps * gaps + smooth_width * smooth_width)


def sigmoid(v):
    return 0.5 * jnp.tanh(0.5 * v) + 0.5


def body(
    members,
    shards,
    lat_hbm,
    emb_hbm,
    wmsg_hbm,
    wout_hbm,
    need_hbm,
    src_hbm,
    dst_hbm,
    count_hbm,
    target_hbm,
    pw_hbm,
    fw_hbm,
    out,
    lat,
    emb,
    wmsg,
    wout,
    need,
    src,
    dst,
    count,
    truth,
    pw,
    fw,
    nbr,
    pre,
    od,
    odt,
    n_lr,
    nt,
    summed,
    total16,
    inv,
    fields,
    ens,
    gsend,
    gf,
    w2,
    u,
    grad,
    rsend,
    own,
    back,
    pwcol,
    load_sem,
    lat_send,
    lat_recv,
    ens_send,
    ens_recv,
    gf_send,
    gf_recv,
    back_send,
    back_recv,
    relay,
):
    node_dev, width = lat.shape
    points = emb.shape[0]
    edges = src.shape[0]
    slots = need.shape[1]
    share = points // members
    chunk = 256
    chunks = width // chunk
    me = lax.axis_index("member")
    g = lax.axis_index("grid")
    left = lax.rem(g + shards - 1, shards)
    right = lax.rem(g + 1, shards)
    rows_me = pl.ds(pl.multiple_of(me * share, share), share)

    order = sorted(range(1, members), key=lambda d: -min(d, members - d))

    def ring(d):
        return lax.rem(me + members + d, members)

    def cols(c):
        return pl.ds(c * chunk, chunk)

    barrier = pltpu.get_barrier_semaphore()
    for neighbour in (left, right):
        pl.semaphore_signal(barrier, inc=1, device_id={"grid": neighbour}, device_id_type=MESH)
    mate = me + 1 - 2 * lax.rem(me, 2)
    for other in (mate, ring(2), ring(-2)):
        pl.semaphore_signal(barrier, inc=1, device_id={"member": other}, device_id_type=MESH)

    loads = []
    for source, target in (
        (src_hbm, src),
        (dst_hbm, dst),
        (need_hbm, need),
        (count_hbm, count),
        (lat_hbm.at[0], lat),
        (emb_hbm, emb),
        (wmsg_hbm, wmsg),
        (wout_hbm, wout),
        (pw_hbm, pw),
        (fw_hbm, fw),
        (target_hbm.at[rows_me], truth),
    ):
        copy = pltpu.make_async_copy(source, target, load_sem.at[len(loads)])
        copy.start()
        loads.append(copy)

    for copy in loads[:4]:
        copy.wait()
    lane = lax.broadcasted_iota(jnp.int32, (1, edges), 1)
    dest = jnp.where(lane < count[0], dst[...].reshape(1, edges), -1)
    source = src[...].reshape(1, edges)
    odt[...] = onehot(lax.broadcasted_iota(jnp.int32, (points, edges), 0) == dest)
    dest_col = jnp.transpose(jnp.broadcast_to(dest, (128, edges)))
    lanes = lax.broadcasted_iota(jnp.int32, (edges, 128), 1)
    for first in range(0, points, 128):
        od[:, first : first + 128] = onehot(dest_col == lanes + first)
    os_t = onehot(lax.broadcasted_iota(jnp.int32, (128, edges), 0) == source)
    os_n = onehot(jnp.transpose(jnp.broadcast_to(source, (128, edges))) == lanes)
    code = jnp.concatenate(
        [
            need[0:1, :],
            need[1:2, :] + 2 * node_dev,
            need[2:3, :] + node_dev,
            jnp.full((1, 128 - 3 * slots), -1, jnp.int32),
        ],
        axis=1,
    )
    place = onehot(lax.broadcasted_iota(jnp.int32, (3 * node_dev, 128), 0) == code)
    nt[...] = dot(place, os_t).astype(BF16)
    n_lr[...] = dot(os_n, place[: 2 * node_dev], NT).astype(BF16)
    n_own = dot(os_n, place[2 * node_dev :], NT).astype(BF16)

    loads[4].wait()
    pl.semaphore_wait(barrier, 5)
    lat_copies = []
    for c in range(chunks):
        for side, neighbour in ((1, left), (0, right)):
            copy = pltpu.make_async_remote_copy(
                src_ref=lat.at[:, cols(c)],
                dst_ref=nbr.at[pl.ds(side * node_dev, node_dev), cols(c)],
                send_sem=lat_send.at[side, c],
                recv_sem=lat_recv.at[side, c],
                device_id={"grid": neighbour},
                device_id_type=MESH,
            )
            copy.start()
            lat_copies.append(copy)

    for other in (ring(2), ring(-2)):
        pl.semaphore_signal(relay.at[0], inc=1, device_id={"member": other}, device_id_type=MESH)
    loads[5].wait()
    for c in range(chunks):
        pre[:, cols(c)] = dot(od[...], emb[:, cols(c)]) + dot(n_own, lat[:, cols(c)])
    pl.semaphore_wait(relay.at[0], 2)
    for other in (ring(4), ring(-4)):
        pl.semaphore_signal(relay.at[1], inc=1, device_id={"member": other}, device_id_type=MESH)
    loads[6].wait()
    loads[7].wait()
    product = jnp.transpose(dot(wmsg[...], wout[...]))
    high = product.astype(BF16)
    w2[: high.shape[0], :] = high
    w2[high.shape[0] :, :] = (product - high.astype(F32)).astype(BF16)
    for copy in loads[8:]:
        copy.wait()
    pwcol[...] = jnp.transpose(jnp.broadcast_to(pw[...].reshape(1, points), (128, points)))

    pl.semaphore_wait(relay.at[1], 2)
    pl.semaphore_signal(relay.at[2], inc=1, device_id={"member": mate}, device_id_type=MESH)

    for c in range(chunks):
        for copy in lat_copies[2 * c : 2 * c + 2]:
            copy.wait_recv()
        v = pre[:, cols(c)] + dot(n_lr[...], nbr[:, cols(c)])
        pre[:, cols(c)] = v
        hidden = (v * sigmoid(v)).astype(BF16)
        gathered = dot(odt[...], hidden).astype(BF16)
        part = dot(gathered, wmsg[cols(c), :])
        if c == 0:
            summed[...] = part
        else:
            summed[...] += part
    total = summed[...]
    total16[...] = total.astype(BF16)
    inv_rms = lax.rsqrt(jnp.mean(total * total, axis=1, keepdims=True) + norm_eps)
    fields[...] = dot(total16[...], wout[...]) * inv_rms
    inv[...] = inv_rms

    pl.semaphore_wait(relay.at[2], 1)
    ens_copies = []
    for d in order:
        other = lax.rem(me + d, members)
        copy = pltpu.make_async_remote_copy(
            src_ref=fields.at[pl.ds(pl.multiple_of(other * share, share), share)],
            dst_ref=ens.at[d - 1],
            send_sem=ens_send.at[d - 1],
            recv_sem=ens_recv.at[d - 1],
            device_id={"member": other},
            device_id_type=MESH,
        )
        copy.start()
        ens_copies.append(copy)

    for c in range(chunks):
        v = pre[:, cols(c)]
        s = sigmoid(v)
        pre[:, cols(c)] = s * (1.0 + v * (1.0 - s))
    inv_rms = inv[...]
    u[...] = dot(total16[...], wmsg[...], NT) * (inv_rms * inv_rms)

    weights = pwcol[rows_me, :] * fw[...].reshape(1, fw.shape[0])
    for copy in ens_copies:
        copy.wait_recv()
    x = [fields[rows_me, :]] + [ens[d] for d in range(members - 1)]
    pair = [jnp.zeros_like(x[0]) for _ in x]
    for i in range(members):
        for j in range(i):
            slope = smooth_slope(x[i] - x[j])
            pair[i] = pair[i] + slope
            pair[j] = pair[j] - slope
    y = truth[...]
    grads = [
        (weights * (smooth_slope(x[i] - y) - pair[i] * (1.0 / (members - 1)))).astype(BF16)
        for i in range(members)
    ]
    gf_copies = []
    for d in order:
        gsend[d - 1] = grads[d]
        copy = pltpu.make_async_remote_copy(
            src_ref=gsend.at[d - 1],
            dst_ref=gf.at[rows_me],
            send_sem=gf_send.at[d - 1],
            recv_sem=gf_recv.at[d - 1],
            device_id={"member": lax.rem(me + members - d, members)},
            device_id_type=MESH,
        )
        copy.start()
        gf_copies.append(copy)
    gf[rows_me, :] = grads[0]
    for copy in gf_copies:
        copy.wait_recv()

    got = gf[...]
    along = jnp.sum(got.astype(F32) * fields[...], axis=1, keepdims=True) * (1.0 / width)
    twice = jnp.concatenate([got, got], axis=1)
    inv_rms = inv[...]
    grad[...] = (inv_rms * dot(twice, w2[...]) - along * u[...]).astype(BF16)
    back_copies = []
    ahead = dot(od[...], grad[:, cols(0)])
    for c in range(chunks):
        spread = ahead
        if c + 1 < chunks:
            ahead = dot(od[...], grad[:, cols(c + 1)])
        grad_pre = (spread * pre[:, cols(c)]).astype(BF16)
        rows = dot(nt[...], grad_pre)
        rsend[:, cols(c)] = rows[: 2 * node_dev].astype(BF16)
        own[:, cols(c)] = rows[2 * node_dev :]
        for side, neighbour in ((0, left), (1, right)):
            copy = pltpu.make_async_remote_copy(
                src_ref=rsend.at[pl.ds(side * node_dev, node_dev), cols(c)],
                dst_ref=back.at[side, :, cols(c)],
                send_sem=back_send.at[side, c],
                recv_sem=back_recv.at[side, c],
                device_id={"grid": neighbour},
                device_id_type=MESH,
            )
            copy.start()
            back_copies.append(copy)
    for c in range(chunks):
        for copy in back_copies[2 * c : 2 * c + 2]:
            copy.wait_recv()
        out[0, :, cols(c)] = (
            own[:, cols(c)] + back[0, :, cols(c)].astype(F32) + back[1, :, cols(c)].astype(F32)
        )
    for copy in lat_copies + ens_copies + gf_copies + back_copies:
        copy.wait_send()


def local(
    latents,
    dst_embed,
    w_msg,
    w_out,
    need_rows,
    edge_src,
    edge_dst,
    edge_count,
    target,
    point_weight,
    field_weight,
):
    members = lax.axis_size("member")
    shards = lax.axis_size("grid")
    node_dev, width = latents.shape[1:]
    points = dst_embed.shape[0]
    edges = edge_src.shape[0]
    fields = w_out.shape[1]
    share = points // members
    chunks = width // 256
    dma = pltpu.SemaphoreType.DMA
    return pl.pallas_call(
        functools.partial(body, members, shards),
        out_shape=pltpu.VMEM((1, node_dev, width), F32),
        in_specs=[pl.BlockSpec(memory_space=pl.ANY)] * 11,
        out_specs=pl.BlockSpec(memory_space=pltpu.VMEM),
        scratch_shapes=[
            pltpu.VMEM((node_dev, width), BF16),
            pltpu.VMEM((points, width), BF16),
            pltpu.VMEM((width, width), BF16),
            pltpu.VMEM((width, fields), BF16),
            pltpu.VMEM(need_rows.shape, jnp.int32),
            pltpu.VMEM((edges,), jnp.int32),
            pltpu.VMEM((edges,), jnp.int32),
            pltpu.SMEM((1,), jnp.int32),
            pltpu.VMEM((share, fields), F32),
            pltpu.VMEM((points,), F32),
            pltpu.VMEM((fields,), F32),
            pltpu.VMEM((2 * node_dev, width), BF16),
            pltpu.VMEM((edges, width), F32),
            pltpu.VMEM((edges, points), BF16),
            pltpu.VMEM((points, edges), BF16),
            pltpu.VMEM((edges, 2 * node_dev), BF16),
            pltpu.VMEM((3 * node_dev, edges), BF16),
            pltpu.VMEM((points, width), F32),
            pltpu.VMEM((points, width), BF16),
            pltpu.VMEM((points, 1), F32),
            pltpu.VMEM((points, fields), F32),
            pltpu.VMEM((members - 1, share, fields), F32),
            pltpu.VMEM((members - 1, share, fields), BF16),
            pltpu.VMEM((points, fields), BF16),
            pltpu.VMEM((2 * fields, width), BF16),
            pltpu.VMEM((points, width), F32),
            pltpu.VMEM((points, width), BF16),
            pltpu.VMEM((2 * node_dev, width), BF16),
            pltpu.VMEM((node_dev, width), F32),
            pltpu.VMEM((2, node_dev, width), BF16),
            pltpu.VMEM((points, 128), F32),
            dma((11,)),
            dma((2, chunks)),
            dma((2, chunks)),
            dma((members - 1,)),
            dma((members - 1,)),
            dma((members - 1,)),
            dma((members - 1,)),
            dma((2, chunks)),
            dma((2, chunks)),
            pltpu.SemaphoreType.REGULAR((3,)),
        ],
        compiler_params=pltpu.CompilerParams(
            collective_id=0, has_side_effects=True, vmem_limit_bytes=32 * 1024 * 1024
        ),
        cost_estimate=pl.CostEstimate(
            flops=6_000_000_000, bytes_accessed=4_000_000, transcendentals=1_600_000
        ),
    )(
        pltpu.with_memory_space_constraint(latents, pltpu.HBM),
        pltpu.with_memory_space_constraint(dst_embed, pltpu.HBM),
        pltpu.with_memory_space_constraint(w_msg, pltpu.HBM),
        pltpu.with_memory_space_constraint(w_out, pltpu.HBM),
        pltpu.with_memory_space_constraint(need_rows, pltpu.HBM),
        pltpu.with_memory_space_constraint(edge_src, pltpu.HBM),
        pltpu.with_memory_space_constraint(edge_dst, pltpu.HBM),
        edge_count,
        pltpu.with_memory_space_constraint(target, pltpu.HBM),
        pltpu.with_memory_space_constraint(point_weight, pltpu.HBM),
        pltpu.with_memory_space_constraint(field_weight, pltpu.HBM),
    )


def solution(mesh):
    placed = (
        P("member", "grid", None),
        P("grid", None),
        P(),
        P(),
        P("grid", None),
        P("grid"),
        P("grid"),
        P("grid"),
        P("grid", None),
        P("grid"),
        P(),
    )
    return jax.shard_map(
        local, mesh=mesh, in_specs=placed, out_specs=P("member", "grid", None), check_vma=False
    )
```

```python
import functools

import jax
import jax.numpy as jnp
from jax import lax
from jax.experimental import pallas as pl
from jax.experimental.pallas import tpu as pltpu
from jax.sharding import PartitionSpec as P

smooth_width = 0.1
norm_eps = 1e-06

MESH = pl.DeviceIdType.MESH
NN = (((1,), (0,)), ((), ()))
NT = (((1,), (1,)), ((), ()))
F32 = jnp.float32
BF16 = jnp.bfloat16


def dot(a, b, dims=NN):
    return lax.dot_general(a, b, dims, preferred_element_type=F32)


def onehot(condition):
    return jnp.where(condition, 1.0, 0.0).astype(BF16)


def smooth_slope(gaps):
    return gaps * lax.rsqrt(gaps * gaps + smooth_width * smooth_width)


def sigmoid(v):
    return 0.5 * jnp.tanh(0.5 * v) + 0.5


def body(
    members,
    shards,
    lat_hbm,
    emb_hbm,
    wmsg_hbm,
    wout_hbm,
    need_hbm,
    src_hbm,
    dst_hbm,
    count_hbm,
    target_hbm,
    pw_hbm,
    fw_hbm,
    out,
    lat,
    emb,
    wmsg,
    wout,
    need,
    src,
    dst,
    count,
    truth,
    pw,
    fw,
    nbr,
    pre,
    od,
    odt,
    n_lr,
    nt,
    gathered,
    summed,
    total16,
    inv,
    fields,
    ens,
    fields16,
    gsend,
    gf,
    w2,
    u,
    rsend,
    own,
    back,
    pwcol,
    load_sem,
    lat_send,
    lat_recv,
    ens_send,
    ens_recv,
    gf_send,
    gf_recv,
    back_send,
    back_recv,
    relay,
):
    node_dev, width = lat.shape
    points = emb.shape[0]
    edges = src.shape[0]
    slots = need.shape[1]
    share = points // members
    chunk = 256
    chunks = width // chunk
    me = lax.axis_index("member")
    g = lax.axis_index("grid")
    left = lax.rem(g + shards - 1, shards)
    right = lax.rem(g + 1, shards)
    rows_me = pl.ds(pl.multiple_of(me * share, share), share)

    order = sorted(range(1, members), key=lambda d: -min(d, members - d))

    def arrived(block, sem):
        pltpu.make_async_copy(block, block, sem).wait()

    def ring(d):
        return lax.rem(me + members + d, members)

    def cols(c):
        return pl.ds(c * chunk, chunk)

    barrier = pltpu.get_barrier_semaphore()
    for neighbour in (left, right):
        pl.semaphore_signal(barrier, inc=1, device_id={"grid": neighbour}, device_id_type=MESH)
    mate = me + 1 - 2 * lax.rem(me, 2)
    for other in (mate, ring(2), ring(-2)):
        pl.semaphore_signal(barrier, inc=1, device_id={"member": other}, device_id_type=MESH)

    loads = []
    for source, target in (
        (src_hbm, src),
        (dst_hbm, dst),
        (need_hbm, need),
        (count_hbm, count),
        (lat_hbm.at[0], lat),
        (emb_hbm, emb),
        (wmsg_hbm, wmsg),
        (wout_hbm, wout),
        (pw_hbm, pw),
        (fw_hbm, fw),
        (target_hbm.at[rows_me], truth),
    ):
        copy = pltpu.make_async_copy(source, target, load_sem.at[len(loads)])
        copy.start()
        loads.append(copy)

    for copy in loads[:4]:
        copy.wait()
    lane = lax.broadcasted_iota(jnp.int32, (1, edges), 1)
    dest = jnp.where(lane < count[0], dst[...].reshape(1, edges), -1)
    source = src[...].reshape(1, edges)
    odt[...] = onehot(lax.broadcasted_iota(jnp.int32, (points, edges), 0) == dest)
    dest_col = jnp.transpose(jnp.broadcast_to(dest, (128, edges)))
    lanes = lax.broadcasted_iota(jnp.int32, (edges, 128), 1)
    for first in range(0, points, 128):
        od[:, first : first + 128] = onehot(dest_col == lanes + first)
    os_t = onehot(lax.broadcasted_iota(jnp.int32, (128, edges), 0) == source)
    os_n = onehot(jnp.transpose(jnp.broadcast_to(source, (128, edges))) == lanes)
    code = jnp.concatenate(
        [
            need[0:1, :],
            need[1:2, :] + 2 * node_dev,
            need[2:3, :] + node_dev,
            jnp.full((1, 128 - 3 * slots), -1, jnp.int32),
        ],
        axis=1,
    )
    place = onehot(lax.broadcasted_iota(jnp.int32, (3 * node_dev, 128), 0) == code)
    nt[...] = dot(place, os_t).astype(BF16)
    n_lr[...] = dot(os_n, place[: 2 * node_dev], NT).astype(BF16)
    n_own = dot(os_n, place[2 * node_dev :], NT).astype(BF16)

    loads[4].wait()
    pl.semaphore_wait(barrier, 5)
    lat_copies = []
    for side, neighbour in ((1, left), (0, right)):
        copy = pltpu.make_async_remote_copy(
            src_ref=lat,
            dst_ref=nbr.at[pl.ds(side * node_dev, node_dev)],
            send_sem=lat_send.at[side],
            recv_sem=lat_recv.at[side],
            device_id={"grid": neighbour},
            device_id_type=MESH,
        )
        copy.start()
        lat_copies.append(copy)

    for other in (ring(2), ring(-2)):
        pl.semaphore_signal(relay.at[0], inc=1, device_id={"member": other}, device_id_type=MESH)
    loads[5].wait()
    for c in range(chunks):
        pre[:, cols(c)] = dot(od[...], emb[:, cols(c)]) + dot(n_own, lat[:, cols(c)])
    pl.semaphore_wait(relay.at[0], 2)
    for other in (ring(4), ring(-4)):
        pl.semaphore_signal(relay.at[1], inc=1, device_id={"member": other}, device_id_type=MESH)
    loads[6].wait()
    loads[7].wait()
    pl.semaphore_wait(relay.at[1], 2)
    pl.semaphore_signal(relay.at[2], inc=1, device_id={"member": mate}, device_id_type=MESH)

    def hidden(c):
        v = pre[:, cols(c)] + dot(n_lr[...], nbr[:, cols(c)])
        pre[:, cols(c)] = v
        return (v * sigmoid(v)).astype(BF16)

    for copy in lat_copies:
        copy.wait_recv()
    ahead = hidden(0)
    for c in range(chunks - 1):
        now = ahead
        ahead = hidden(c + 1)
        gathered[:, cols(c)] = dot(odt[...], now).astype(BF16)
    gathered[:, cols(chunks - 1)] = dot(odt[...], ahead).astype(BF16)
    total = dot(gathered[...], wmsg[...])
    total16[...] = total.astype(BF16)
    inv_rms = lax.rsqrt(jnp.mean(total * total, axis=1, keepdims=True) + norm_eps)
    fields[...] = dot(total16[...], wout[...]) * inv_rms
    inv[...] = inv_rms

    pl.semaphore_wait(relay.at[2], 1)
    fields16[...] = fields[...].astype(BF16)
    for d in order:
        other = lax.rem(me + d, members)
        copy = pltpu.make_async_remote_copy(
            src_ref=fields16.at[pl.ds(pl.multiple_of(other * share, share), share)],
            dst_ref=ens.at[d - 1],
            send_sem=ens_send,
            recv_sem=ens_recv,
            device_id={"member": other},
            device_id_type=MESH,
        )
        copy.start()

    for c in range(chunks):
        v = pre[:, cols(c)]
        s = sigmoid(v)
        pre[:, cols(c)] = s * (1.0 + v * (1.0 - s))
    inv_rms = inv[...]
    product = jnp.transpose(dot(wmsg[...], wout[...]))
    high = product.astype(BF16)
    w2[: high.shape[0], :] = high
    w2[high.shape[0] :, :] = (product - high.astype(F32)).astype(BF16)
    for copy in loads[8:]:
        copy.wait()
    pwcol[...] = jnp.transpose(jnp.broadcast_to(pw[...].reshape(1, points), (128, points)))

    u[...] = dot(total16[...], wmsg[...], NT) * (inv_rms * inv_rms)

    weights = pwcol[rows_me, :] * fw[...].reshape(1, fw.shape[0])
    for copy in lat_copies:
        copy.wait_send()
    arrived(ens, ens_recv)
    x = [fields16[rows_me, :].astype(F32)] + [ens[d].astype(F32) for d in range(members - 1)]
    pair = [jnp.zeros_like(x[0]) for _ in x]
    for i in range(members):
        for j in range(i):
            slope = smooth_slope(x[i] - x[j])
            pair[i] = pair[i] + slope
            pair[j] = pair[j] - slope
    y = truth[...]
    grads = [
        (weights * (smooth_slope(x[i] - y) - pair[i] * (1.0 / (members - 1)))).astype(BF16)
        for i in range(members)
    ]
    for d in order:
        gsend[d - 1] = grads[d]
        copy = pltpu.make_async_remote_copy(
            src_ref=gsend.at[d - 1],
            dst_ref=gf.at[rows_me],
            send_sem=gf_send,
            recv_sem=gf_recv,
            device_id={"member": lax.rem(me + members - d, members)},
            device_id_type=MESH,
        )
        copy.start()
    gf[rows_me, :] = grads[0]
    arrived(ens, ens_send)
    arrived(gsend, gf_recv)

    got = gf[...]
    along = jnp.sum(got.astype(F32) * fields[...], axis=1, keepdims=True) * (1.0 / width)
    twice = jnp.concatenate([got, got], axis=1)
    inv_rms = inv[...]

    def point_grads(c):
        return (inv_rms * dot(twice, w2[:, cols(c)]) - along * u[:, cols(c)]).astype(BF16)

    back_copies = []
    ahead = dot(od[...], point_grads(0))
    grad = point_grads(1)
    for c in range(chunks):
        spread = ahead
        if c + 1 < chunks:
            ahead = dot(od[...], grad)
        if c + 2 < chunks:
            grad = point_grads(c + 2)
        grad_pre = (spread * pre[:, cols(c)]).astype(BF16)
        rows = dot(nt[...], grad_pre)
        rsend[:, cols(c)] = rows[: 2 * node_dev].astype(BF16)
        own[:, cols(c)] = rows[2 * node_dev :]
        for side, neighbour in ((0, left), (1, right)):
            copy = pltpu.make_async_remote_copy(
                src_ref=rsend.at[pl.ds(side * node_dev, node_dev), cols(c)],
                dst_ref=back.at[side, :, cols(c)],
                send_sem=back_send.at[side, c],
                recv_sem=back_recv.at[side, c],
                device_id={"grid": neighbour},
                device_id_type=MESH,
            )
            copy.start()
            back_copies.append(copy)
    arrived(gsend, gf_send)
    for c in range(chunks):
        for copy in back_copies[2 * c : 2 * c + 2]:
            copy.wait_recv()
        out[0, :, cols(c)] = (
            own[:, cols(c)] + back[0, :, cols(c)].astype(F32) + back[1, :, cols(c)].astype(F32)
        )
    for copy in back_copies:
        copy.wait_send()


def local(
    latents,
    dst_embed,
    w_msg,
    w_out,
    need_rows,
    edge_src,
    edge_dst,
    edge_count,
    target,
    point_weight,
    field_weight,
):
    members = lax.axis_size("member")
    shards = lax.axis_size("grid")
    node_dev, width = latents.shape[1:]
    points = dst_embed.shape[0]
    edges = edge_src.shape[0]
    fields = w_out.shape[1]
    share = points // members
    chunks = width // 256
    dma = pltpu.SemaphoreType.DMA
    return pl.pallas_call(
        functools.partial(body, members, shards),
        out_shape=pltpu.VMEM((1, node_dev, width), F32),
        in_specs=[pl.BlockSpec(memory_space=pl.ANY)] * 11,
        out_specs=pl.BlockSpec(memory_space=pltpu.VMEM),
        scratch_shapes=[
            pltpu.VMEM((node_dev, width), BF16),
            pltpu.VMEM((points, width), BF16),
            pltpu.VMEM((width, width), BF16),
            pltpu.VMEM((width, fields), BF16),
            pltpu.VMEM(need_rows.shape, jnp.int32),
            pltpu.VMEM((edges,), jnp.int32),
            pltpu.VMEM((edges,), jnp.int32),
            pltpu.SMEM((1,), jnp.int32),
            pltpu.VMEM((share, fields), F32),
            pltpu.VMEM((points,), F32),
            pltpu.VMEM((fields,), F32),
            pltpu.VMEM((2 * node_dev, width), BF16),
            pltpu.VMEM((edges, width), F32),
            pltpu.VMEM((edges, points), BF16),
            pltpu.VMEM((points, edges), BF16),
            pltpu.VMEM((edges, 2 * node_dev), BF16),
            pltpu.VMEM((3 * node_dev, edges), BF16),
            pltpu.VMEM((points, width), BF16),
            pltpu.VMEM((points, width), F32),
            pltpu.VMEM((points, width), BF16),
            pltpu.VMEM((points, 1), F32),
            pltpu.VMEM((points, fields), F32),
            pltpu.VMEM((members - 1, share, fields), BF16),
            pltpu.VMEM((points, fields), BF16),
            pltpu.VMEM((members - 1, share, fields), BF16),
            pltpu.VMEM((points, fields), BF16),
            pltpu.VMEM((2 * fields, width), BF16),
            pltpu.VMEM((points, width), F32),
            pltpu.VMEM((2 * node_dev, width), BF16),
            pltpu.VMEM((node_dev, width), F32),
            pltpu.VMEM((2, node_dev, width), BF16),
            pltpu.VMEM((points, 128), F32),
            dma((11,)),
            dma((2,)),
            dma((2,)),
            dma,
            dma,
            dma,
            dma,
            dma((2, chunks)),
            dma((2, chunks)),
            pltpu.SemaphoreType.REGULAR((3,)),
        ],
        compiler_params=pltpu.CompilerParams(
            collective_id=0, has_side_effects=True, vmem_limit_bytes=32 * 1024 * 1024
        ),
        cost_estimate=pl.CostEstimate(
            flops=6_000_000_000, bytes_accessed=4_000_000, transcendentals=1_600_000
        ),
    )(
        pltpu.with_memory_space_constraint(latents, pltpu.HBM),
        pltpu.with_memory_space_constraint(dst_embed, pltpu.HBM),
        pltpu.with_memory_space_constraint(w_msg, pltpu.HBM),
        pltpu.with_memory_space_constraint(w_out, pltpu.HBM),
        pltpu.with_memory_space_constraint(need_rows, pltpu.HBM),
        pltpu.with_memory_space_constraint(edge_src, pltpu.HBM),
        pltpu.with_memory_space_constraint(edge_dst, pltpu.HBM),
        edge_count,
        pltpu.with_memory_space_constraint(target, pltpu.HBM),
        pltpu.with_memory_space_constraint(point_weight, pltpu.HBM),
        pltpu.with_memory_space_constraint(field_weight, pltpu.HBM),
    )


def solution(mesh):
    placed = (
        P("member", "grid", None),
        P("grid", None),
        P(),
        P(),
        P("grid", None),
        P("grid"),
        P("grid"),
        P("grid"),
        P("grid", None),
        P("grid"),
        P(),
    )
    return jax.shard_map(
        local, mesh=mesh, in_specs=placed, out_specs=P("member", "grid", None), check_vma=False
    )
```

```python
import functools

import jax
import jax.numpy as jnp
from jax import lax
from jax.experimental import pallas as pl
from jax.experimental.pallas import tpu as pltpu
from jax.sharding import PartitionSpec as P

smooth_width = 0.1
norm_eps = 1e-06

MESH = pl.DeviceIdType.MESH
NN = (((1,), (0,)), ((), ()))
NT = (((1,), (1,)), ((), ()))
F32 = jnp.float32
BF16 = jnp.bfloat16


def dot(a, b, dims=NN):
    return lax.dot_general(a, b, dims, preferred_element_type=F32)


def onehot(condition):
    return jnp.where(condition, 1.0, 0.0).astype(BF16)


def smooth_slope(gaps):
    return gaps * lax.rsqrt(gaps * gaps + smooth_width * smooth_width)


def sigmoid(v):
    return 0.5 * jnp.tanh(0.5 * v) + 0.5


def body(
    members,
    shards,
    lat_hbm,
    emb_hbm,
    wmsg_hbm,
    wout_hbm,
    need_hbm,
    src_hbm,
    dst_hbm,
    count_hbm,
    target_hbm,
    pw_hbm,
    fw_hbm,
    out,
    lat,
    emb,
    wmsg,
    wout,
    need,
    src,
    dst,
    count,
    truth,
    pw,
    fw,
    need_nbr,
    put,
    nbr,
    pre,
    od,
    odt,
    n_lr,
    nt,
    gathered,
    summed,
    total16,
    inv,
    fields,
    ens,
    fields16,
    gsend,
    gf,
    w2,
    u,
    rsend,
    own,
    back,
    pwcol,
    load_sem,
    lat_send,
    lat_recv,
    need_send,
    need_recv,
    ens_send,
    ens_recv,
    gf_send,
    gf_recv,
    back_send,
    back_recv,
    relay,
):
    node_dev, width = lat.shape
    points = emb.shape[0]
    edges = src.shape[0]
    slots = need.shape[1]
    share = points // members
    chunk = 256
    chunks = width // chunk
    me = lax.axis_index("member")
    g = lax.axis_index("grid")
    left = lax.rem(g + shards - 1, shards)
    right = lax.rem(g + 1, shards)
    rows_me = pl.ds(pl.multiple_of(me * share, share), share)

    order = sorted(range(1, members), key=lambda d: -min(d, members - d))

    def arrived(block, sem):
        pltpu.make_async_copy(block, block, sem).wait()

    def ring(d):
        return lax.rem(me + members + d, members)

    def cols(c):
        return pl.ds(c * chunk, chunk)

    barrier = pltpu.get_barrier_semaphore()
    for neighbour in (left, right):
        pl.semaphore_signal(barrier, inc=1, device_id={"grid": neighbour}, device_id_type=MESH)
    mate = me + 1 - 2 * lax.rem(me, 2)
    for other in (mate, ring(2), ring(-2)):
        pl.semaphore_signal(barrier, inc=1, device_id={"member": other}, device_id_type=MESH)

    loads = []
    for source, target in (
        (src_hbm, src),
        (dst_hbm, dst),
        (need_hbm, need),
        (count_hbm, count),
        (lat_hbm.at[0], lat),
        (emb_hbm, emb),
        (wmsg_hbm, wmsg),
        (wout_hbm, wout),
        (pw_hbm, pw),
        (fw_hbm, fw),
        (target_hbm.at[rows_me], truth),
    ):
        copy = pltpu.make_async_copy(source, target, load_sem.at[len(loads)])
        copy.start()
        loads.append(copy)

    loads[4].wait()
    pl.semaphore_wait(barrier, 5)
    lat_copies = []
    for side, neighbour in ((1, left), (0, right)):
        copy = pltpu.make_async_remote_copy(
            src_ref=lat,
            dst_ref=nbr.at[pl.ds(side * node_dev, node_dev)],
            send_sem=lat_send.at[side],
            recv_sem=lat_recv.at[side],
            device_id={"grid": neighbour},
            device_id_type=MESH,
        )
        copy.start()
        lat_copies.append(copy)

    loads[2].wait()
    need_copies = []
    for side, neighbour in ((1, left), (0, right)):
        copy = pltpu.make_async_remote_copy(
            src_ref=need,
            dst_ref=need_nbr.at[side],
            send_sem=need_send.at[side],
            recv_sem=need_recv.at[side],
            device_id={"grid": neighbour},
            device_id_type=MESH,
        )
        copy.start()
        need_copies.append(copy)

    for other in (ring(2), ring(-2)):
        pl.semaphore_signal(relay.at[0], inc=1, device_id={"member": other}, device_id_type=MESH)
    for copy in loads[:2] + loads[3:4]:
        copy.wait()
    lane = lax.broadcasted_iota(jnp.int32, (1, edges), 1)
    dest = jnp.where(lane < count[0], dst[...].reshape(1, edges), -1)
    source = src[...].reshape(1, edges)
    odt[...] = onehot(lax.broadcasted_iota(jnp.int32, (points, edges), 0) == dest)
    dest_col = jnp.transpose(jnp.broadcast_to(dest, (128, edges)))
    lanes = lax.broadcasted_iota(jnp.int32, (edges, 128), 1)
    for first in range(0, points, 128):
        od[:, first : first + 128] = onehot(dest_col == lanes + first)
    os_t = onehot(lax.broadcasted_iota(jnp.int32, (128, edges), 0) == source)
    os_n = onehot(jnp.transpose(jnp.broadcast_to(source, (128, edges))) == lanes)
    code = jnp.concatenate(
        [
            need[0:1, :],
            need[1:2, :] + 2 * node_dev,
            need[2:3, :] + node_dev,
            jnp.full((1, 128 - 3 * slots), -1, jnp.int32),
        ],
        axis=1,
    )
    place = onehot(lax.broadcasted_iota(jnp.int32, (3 * node_dev, 128), 0) == code)
    nt[:slots, :] = os_t[:slots]
    nt[slots : 2 * slots, :] = os_t[2 * slots : 3 * slots]
    nt[2 * slots :, :] = dot(place[2 * node_dev :], os_t).astype(BF16)
    n_lr[...] = dot(os_n, place[: 2 * node_dev], NT).astype(BF16)
    n_own = dot(os_n, place[2 * node_dev :], NT).astype(BF16)

    loads[5].wait()
    for c in range(chunks):
        pre[:, cols(c)] = dot(od[...], emb[:, cols(c)]) + dot(n_own, lat[:, cols(c)])
    pl.semaphore_wait(relay.at[0], 2)
    for other in (ring(4), ring(-4)):
        pl.semaphore_signal(relay.at[1], inc=1, device_id={"member": other}, device_id_type=MESH)
    loads[6].wait()
    loads[7].wait()
    pl.semaphore_wait(relay.at[1], 2)
    pl.semaphore_signal(relay.at[2], inc=1, device_id={"member": mate}, device_id_type=MESH)

    def hidden(c):
        v = pre[:, cols(c)] + dot(n_lr[...], nbr[:, cols(c)])
        pre[:, cols(c)] = v
        return (v * sigmoid(v)).astype(BF16)

    for copy in lat_copies:
        copy.wait_recv()
    ahead = hidden(0)
    for c in range(chunks - 1):
        now = ahead
        ahead = hidden(c + 1)
        gathered[:, cols(c)] = dot(odt[...], now).astype(BF16)
    gathered[:, cols(chunks - 1)] = dot(odt[...], ahead).astype(BF16)
    total = dot(gathered[...], wmsg[...])
    total16[...] = total.astype(BF16)
    inv_rms = lax.rsqrt(jnp.mean(total * total, axis=1, keepdims=True) + norm_eps)
    fields[...] = dot(total16[...], wout[...]) * inv_rms
    inv[...] = inv_rms

    pl.semaphore_wait(relay.at[2], 1)
    fields16[...] = fields[...].astype(BF16)
    for d in order:
        other = lax.rem(me + d, members)
        copy = pltpu.make_async_remote_copy(
            src_ref=fields16.at[pl.ds(pl.multiple_of(other * share, share), share)],
            dst_ref=ens.at[d - 1],
            send_sem=ens_send,
            recv_sem=ens_recv,
            device_id={"member": other},
            device_id_type=MESH,
        )
        copy.start()

    for c in range(chunks):
        v = pre[:, cols(c)]
        s = sigmoid(v)
        pre[:, cols(c)] = s * (1.0 + v * (1.0 - s))
    inv_rms = inv[...]
    product = jnp.transpose(dot(wmsg[...], wout[...]))
    high = product.astype(BF16)
    w2[: high.shape[0], :] = high
    w2[high.shape[0] :, :] = (product - high.astype(F32)).astype(BF16)
    for copy in loads[8:]:
        copy.wait()
    pwcol[...] = jnp.transpose(jnp.broadcast_to(pw[...].reshape(1, points), (128, points)))

    u[...] = dot(total16[...], wmsg[...], NT) * (inv_rms * inv_rms)

    weights = pwcol[rows_me, :] * fw[...].reshape(1, fw.shape[0])
    for copy in lat_copies:
        copy.wait_send()
    arrived(ens, ens_recv)
    x = [fields16[rows_me, :].astype(F32)] + [ens[d].astype(F32) for d in range(members - 1)]
    pair = [jnp.zeros_like(x[0]) for _ in x]
    for i in range(members):
        for j in range(i):
            slope = smooth_slope(x[i] - x[j])
            pair[i] = pair[i] + slope
            pair[j] = pair[j] - slope
    y = truth[...]
    grads = [
        (weights * (smooth_slope(x[i] - y) - pair[i] * (1.0 / (members - 1)))).astype(BF16)
        for i in range(members)
    ]
    for d in order:
        gsend[d - 1] = grads[d]
        copy = pltpu.make_async_remote_copy(
            src_ref=gsend.at[d - 1],
            dst_ref=gf.at[rows_me],
            send_sem=gf_send,
            recv_sem=gf_recv,
            device_id={"member": lax.rem(me + members - d, members)},
            device_id_type=MESH,
        )
        copy.start()
    gf[rows_me, :] = grads[0]
    arrived(ens, ens_send)
    for copy in need_copies:
        copy.wait()
    theirs = jnp.concatenate([need_nbr[0, 2:3, :], need_nbr[1, 0:1, :]], axis=1)
    put[...] = onehot(lax.broadcasted_iota(jnp.int32, (node_dev, 2 * slots), 0) == theirs)
    arrived(gsend, gf_recv)

    got = gf[...]
    along = jnp.sum(got.astype(F32) * fields[...], axis=1, keepdims=True) * (1.0 / width)
    twice = jnp.concatenate([got, got], axis=1)
    inv_rms = inv[...]

    def point_grads(c):
        return (inv_rms * dot(twice, w2[:, cols(c)]) - along * u[:, cols(c)]).astype(BF16)

    back_copies = []
    ahead = dot(od[...], point_grads(0))
    grad = point_grads(1)
    for c in range(chunks):
        spread = ahead
        if c + 1 < chunks:
            ahead = dot(od[...], grad)
        if c + 2 < chunks:
            grad = point_grads(c + 2)
        grad_pre = (spread * pre[:, cols(c)]).astype(BF16)
        rows = dot(nt[...], grad_pre)
        rsend[:, cols(c)] = rows[: 2 * slots].astype(BF16)
        own[:, cols(c)] = rows[2 * slots :]
        for side, neighbour in ((0, left), (1, right)):
            copy = pltpu.make_async_remote_copy(
                src_ref=rsend.at[pl.ds(side * slots, slots), cols(c)],
                dst_ref=back.at[pl.ds((1 - side) * slots, slots), cols(c)],
                send_sem=back_send.at[side, c],
                recv_sem=back_recv.at[side, c],
                device_id={"grid": neighbour},
                device_id_type=MESH,
            )
            copy.start()
            back_copies.append(copy)
    arrived(gsend, gf_send)
    for copy in back_copies:
        copy.wait_recv()
    out[0] = own[...] + dot(put[...], back[...])
    for copy in back_copies:
        copy.wait_send()


def local(
    latents,
    dst_embed,
    w_msg,
    w_out,
    need_rows,
    edge_src,
    edge_dst,
    edge_count,
    target,
    point_weight,
    field_weight,
):
    members = lax.axis_size("member")
    shards = lax.axis_size("grid")
    node_dev, width = latents.shape[1:]
    points = dst_embed.shape[0]
    edges = edge_src.shape[0]
    fields = w_out.shape[1]
    slots = need_rows.shape[1]
    share = points // members
    chunks = width // 256
    dma = pltpu.SemaphoreType.DMA
    return pl.pallas_call(
        functools.partial(body, members, shards),
        out_shape=pltpu.VMEM((1, node_dev, width), F32),
        in_specs=[pl.BlockSpec(memory_space=pl.ANY)] * 11,
        out_specs=pl.BlockSpec(memory_space=pltpu.VMEM),
        scratch_shapes=[
            pltpu.VMEM((node_dev, width), BF16),
            pltpu.VMEM((points, width), BF16),
            pltpu.VMEM((width, width), BF16),
            pltpu.VMEM((width, fields), BF16),
            pltpu.VMEM(need_rows.shape, jnp.int32),
            pltpu.VMEM((edges,), jnp.int32),
            pltpu.VMEM((edges,), jnp.int32),
            pltpu.SMEM((1,), jnp.int32),
            pltpu.VMEM((share, fields), F32),
            pltpu.VMEM((points,), F32),
            pltpu.VMEM((fields,), F32),
            pltpu.VMEM((2,) + need_rows.shape, jnp.int32),
            pltpu.VMEM((node_dev, 2 * slots), BF16),
            pltpu.VMEM((2 * node_dev, width), BF16),
            pltpu.VMEM((edges, width), F32),
            pltpu.VMEM((edges, points), BF16),
            pltpu.VMEM((points, edges), BF16),
            pltpu.VMEM((edges, 2 * node_dev), BF16),
            pltpu.VMEM((2 * slots + node_dev, edges), BF16),
            pltpu.VMEM((points, width), BF16),
            pltpu.VMEM((points, width), F32),
            pltpu.VMEM((points, width), BF16),
            pltpu.VMEM((points, 1), F32),
            pltpu.VMEM((points, fields), F32),
            pltpu.VMEM((members - 1, share, fields), BF16),
            pltpu.VMEM((points, fields), BF16),
            pltpu.VMEM((members - 1, share, fields), BF16),
            pltpu.VMEM((points, fields), BF16),
            pltpu.VMEM((2 * fields, width), BF16),
            pltpu.VMEM((points, width), F32),
            pltpu.VMEM((2 * slots, width), BF16),
            pltpu.VMEM((node_dev, width), F32),
            pltpu.VMEM((2 * slots, width), BF16),
            pltpu.VMEM((points, 128), F32),
            dma((11,)),
            dma((2,)),
            dma((2,)),
            dma((2,)),
            dma((2,)),
            dma,
            dma,
            dma,
            dma,
            dma((2, chunks)),
            dma((2, chunks)),
            pltpu.SemaphoreType.REGULAR((3,)),
        ],
        compiler_params=pltpu.CompilerParams(
            collective_id=0, has_side_effects=True, vmem_limit_bytes=32 * 1024 * 1024
        ),
        cost_estimate=pl.CostEstimate(
            flops=6_000_000_000, bytes_accessed=4_000_000, transcendentals=1_600_000
        ),
    )(
        pltpu.with_memory_space_constraint(latents, pltpu.HBM),
        pltpu.with_memory_space_constraint(dst_embed, pltpu.HBM),
        pltpu.with_memory_space_constraint(w_msg, pltpu.HBM),
        pltpu.with_memory_space_constraint(w_out, pltpu.HBM),
        pltpu.with_memory_space_constraint(need_rows, pltpu.HBM),
        pltpu.with_memory_space_constraint(edge_src, pltpu.HBM),
        pltpu.with_memory_space_constraint(edge_dst, pltpu.HBM),
        edge_count,
        pltpu.with_memory_space_constraint(target, pltpu.HBM),
        pltpu.with_memory_space_constraint(point_weight, pltpu.HBM),
        pltpu.with_memory_space_constraint(field_weight, pltpu.HBM),
    )


def solution(mesh):
    placed = (
        P("member", "grid", None),
        P("grid", None),
        P(),
        P(),
        P("grid", None),
        P("grid"),
        P("grid"),
        P("grid"),
        P("grid", None),
        P("grid"),
        P(),
    )
    return jax.shard_map(
        local, mesh=mesh, in_specs=placed, out_specs=P("member", "grid", None), check_vma=False
    )
```
